256 devices in a mesh: expert: 32 (over y, x, core), replica: 8 (over z).
Axes of the slice: x: 4, y: 4, z: 8, core: 2. Of those that a mesh axis runs over, the one named last changes fastest.
Arguments:
- tokens: bfloat16 [131072, 2048], P(('expert', 'replica')), may hold values from -6 to 6
- d_hidden: bfloat16 [131072, 768], P(('expert', 'replica')), may hold values from -6 to 6
- w_gate: bfloat16 [128, 2048, 768], P(None, ('expert', 'replica')), may hold values from -0.125 to 0.125
- w_up: bfloat16 [128, 2048, 768], P(None, ('expert', 'replica')), may hold values from -0.125 to 0.125
- expert_ids: int32 [256], replicated, may hold values from 0 to 127
Outputs:
- hidden: bfloat16 [131072, 768], P(('expert', 'replica'))
- token_grad: bfloat16 [131072, 2048], P(('expert', 'replica'))
- grad_gate: bfloat16 [128, 2048, 768], P(None, ('expert', 'replica'))
- grad_up: bfloat16 [128, 2048, 768], P(None, ('expert', 'replica'))
The draws below stay inside these ranges and needn't reach their ends.
Inputs may be any that keep to these rules, and one draw needn't show every extreme that they name: expert_ids[b] is the expert used by the rows of block b; several blocks may use the same expert.
All inputs are finite; a program needn't handle non-finite values.
Results may differ from the reference program's by a relative error of at most 0.0057.
Values may be sent and summed in bfloat16 or wider, within the bound.
No kernel may reach another device: no remote copies, remote signals or barrier semaphores. Data moves between devices by JAX's collectives and lax.ppermute only.
A program may use at most 128 MiB of HBM per device.

```python
import math
import jax
import jax.numpy as jnp
import numpy as np
from jax import lax

D = 2048
FF = 768
TOK_DEV = 512
EXPERTS = 128
BLOCKS = 256
ROWS = 131072


def with_ends(result, own_key, low, largest):
    dims = result.shape
    place = [jax.random.randint(jax.random.fold_in(own_key, axis), (), 0, dims[axis]) for axis in range(len(dims))]
    result = result.at[tuple(place)].set(low)
    longest = dims.index(max(dims))
    place[longest] = (place[longest] + 1) % dims[longest]
    return result.at[tuple(place)].set(largest)


def shard_levels(stream_key, dims, pieces, low, largest):
    gain, own = 1.0, jax.random.fold_in(stream_key, 6)
    for position, parts in pieces:
        draws = jnp.exp(jax.random.uniform(jax.random.fold_in(own, position), (parts,), jnp.float32, low / len(pieces), largest / len(pieces)))
        gain = gain * jnp.repeat(draws, dims[position] // parts).reshape([-1 if axis == position else 1 for axis in range(len(dims))])
    return gain


def rank_bounds(number_of, skew):
    loads = [(1 << 20) // math.isqrt(grade ** skew) + 1 for grade in range(1, number_of + 1)]
    spread = 1 + sum(loads) // (1 << 30)
    return np.cumsum(np.array([max(1, weight // spread) for weight in loads]))


def ranked(own_key, shape, number_of, skew):
    table = rank_bounds(number_of, skew)
    pick = jax.random.randint(jax.random.fold_in(own_key, 1), shape, 0, int(table[number_of - 1]))
    grade = jnp.searchsorted(jnp.asarray(table, jnp.int32), pick, side="right")
    return jax.random.permutation(jax.random.fold_in(own_key, 2), number_of)[grade].astype(jnp.int32)


def gaussian(own_key, dims, width, bound, pieces=(), dtype=jnp.bfloat16):
    drawn = width * jax.random.normal(own_key, dims, jnp.float32)
    if pieces:
        drawn = drawn * shard_levels(own_key, dims, pieces, -0.22, 0.18)
    return jnp.clip(drawn, -bound, bound).astype(dtype)


def setup_inputs(seed: int = 0) -> dict:
    arg_keys = jax.random.split(jax.random.key(seed), 6)
    return {
        "tokens": gaussian(arg_keys[0], (ROWS, D), 1.0, 6.0, ((0, 256),)),
        "d_hidden": gaussian(arg_keys[1], (ROWS, FF), 1.0, 6.0, ((0, 256),)),
        "w_gate": gaussian(arg_keys[2], (EXPERTS, D, FF), D ** -0.5, 0.125, ((1, 256),)),
        "w_up": gaussian(arg_keys[3], (EXPERTS, D, FF), D ** -0.5, 0.125, ((1, 256),)),
        "expert_ids": with_ends(ranked(arg_keys[4], (BLOCKS,), EXPERTS, 2), jax.random.fold_in(arg_keys[4], 3), 0, EXPERTS - 1).astype(jnp.int32),
    }


def reference(tokens, d_hidden, w_gate, w_up, expert_ids):
    count = expert_ids.shape[0]
    token_blocks = tokens.reshape(count, TOK_DEV, D)
    grad_blocks = d_hidden.reshape(count, TOK_DEV, FF)
    scale = TOK_DEV ** -0.5

    def step(carry, item):
        acc_gate, acc_up = carry
        rows, upstream_bf, which = item
        gate_whole = w_gate[which]
        up_whole = w_up[which]
        gate_pre = jnp.dot(rows, gate_whole, preferred_element_type=jnp.float32)
        up_pre = jnp.dot(rows, up_whole, preferred_element_type=jnp.float32)
        sigmoid_gate = jax.nn.sigmoid(gate_pre)
        activated = gate_pre * sigmoid_gate
        hidden_block = (activated * up_pre).astype(jnp.bfloat16)
        upstream = upstream_bf.astype(jnp.float32)
        d_gate = (upstream * up_pre * sigmoid_gate * (1.0 + gate_pre * (1.0 - sigmoid_gate))).astype(jnp.bfloat16)
        d_up = (upstream * activated).astype(jnp.bfloat16)
        token_block = (jnp.dot(d_gate, gate_whole.T, preferred_element_type=jnp.float32)
                       + jnp.dot(d_up, up_whole.T, preferred_element_type=jnp.float32)).astype(jnp.bfloat16)
        part_gate = jnp.dot(rows.T, d_gate, preferred_element_type=jnp.float32).astype(jnp.bfloat16)
        part_up = jnp.dot(rows.T, d_up, preferred_element_type=jnp.float32).astype(jnp.bfloat16)
        part_gate = lax.optimization_barrier(part_gate).astype(jnp.float32)
        part_up = lax.optimization_barrier(part_up).astype(jnp.float32)
        acc_gate = lax.dynamic_update_index_in_dim(acc_gate, acc_gate[which] + part_gate, which, 0)
        acc_up = lax.dynamic_update_index_in_dim(acc_up, acc_up[which] + part_up, which, 0)
        return (acc_gate, acc_up), (hidden_block, token_block)

    start = (jnp.zeros(w_gate.shape, jnp.float32), jnp.zeros(w_up.shape, jnp.float32))
    (acc_gate, acc_up), (hidden_blocks, token_blocks_out) = lax.scan(
        step, start, (token_blocks, grad_blocks, expert_ids))
    hidden = hidden_blocks.reshape(tokens.shape[0], FF)
    token_grad = token_blocks_out.reshape(tokens.shape[0], D)
    grad_gate = (acc_gate * scale).astype(jnp.bfloat16)
    grad_up = (acc_up * scale).astype(jnp.bfloat16)
    return hidden, token_grad, grad_gate, grad_up
```

```python
import jax
import jax.numpy as jnp
from jax import lax
from jax.sharding import PartitionSpec as P

BOTH = ("expert", "replica")


def exchange(parts):
    return lax.all_to_all(parts, BOTH, split_axis=0, concat_axis=0, tiled=True)


def per_device(tokens, d_hidden, w_gate, w_up, expert_ids):
    expert_total, block_rows, width = w_gate.shape
    block_count = expert_ids.shape[0]
    model_width = block_count * block_rows
    both = jnp.concatenate([w_gate, w_up], axis=2)
    outgoing = both.at[expert_ids].get(mode="promise_in_bounds")
    weights = exchange(outgoing).reshape(model_width, 2 * width)
    pre = jnp.dot(tokens, weights, preferred_element_type=jnp.float32)
    gate_pre, up_pre = pre[:, :width], pre[:, width:]
    sig = jax.nn.sigmoid(gate_pre)
    activated = gate_pre * sig
    hidden = (activated * up_pre).astype(jnp.bfloat16)
    upstream = d_hidden.astype(jnp.float32)
    d_gate = upstream * up_pre * sig * (1.0 + gate_pre * (1.0 - sig))
    d_up = upstream * activated
    d_both = jnp.concatenate([d_gate, d_up], axis=1).astype(jnp.bfloat16)
    part = lax.dot_general(
        tokens, d_both, (((0,), (0,)), ((), ())), preferred_element_type=jnp.float32
    ).astype(jnp.bfloat16)
    terms = exchange(part.reshape(block_count, block_rows, 2 * width))
    token_grad = lax.dot_general(
        d_both, weights, (((1,), (1,)), ((), ())), preferred_element_type=jnp.float32
    ).astype(jnp.bfloat16)
    selector = (expert_ids[None, :] == jnp.arange(expert_total, dtype=jnp.int32)[:, None]).astype(jnp.bfloat16)
    scale = tokens.shape[0] ** (-0.5)
    grad = jnp.dot(selector, terms.reshape(block_count, -1), preferred_element_type=jnp.float32) * scale
    grad = grad.astype(jnp.bfloat16).reshape(expert_total, block_rows, 2 * width)
    return hidden, token_grad, grad[:, :, :width], grad[:, :, width:]


def solution(mesh):
    rows, weights = P(BOTH, None), P(None, BOTH, None)
    return jax.shard_map(
        per_device,
        mesh=mesh,
        in_specs=(rows, rows, weights, weights, P()),
        out_specs=(rows, rows, weights, weights),
        check_vma=False,
    )
```

```python
import jax
import jax.numpy as jnp
from jax import lax
from jax.experimental import pallas as pl
from jax.experimental.pallas import tpu as pltpu
from jax.sharding import PartitionSpec as P

BOTH = ("expert", "replica")
F32, BF16 = jnp.float32, jnp.bfloat16
MIB = 1 << 20


def each(n, body, unroll=1):
    def step(s, carry):
        body(s)
        return carry

    lax.fori_loop(0, n, step, 0, unroll=unroll)


def gather_rows(ids, w_gate, w_up):
    experts, r, width = w_gate.shape
    blocks = ids.shape[0]
    steps = 4
    share = blocks // steps

    def body(ids, gate, up, out):
        first = pl.program_id(0) * share

        def one(b):
            j = ids[first + b]
            out[b, :, :width] = gate[j]
            out[b, :, width:] = up[j]

        each(share, one, 4)

    whole = pl.BlockSpec((experts, r, width), lambda i, ids: (0, 0, 0))
    return pl.pallas_call(
        body,
        out_shape=jax.ShapeDtypeStruct((blocks, r, 2 * width), BF16),
        grid_spec=pltpu.PrefetchScalarGridSpec(
            num_scalar_prefetch=1,
            grid=(steps,),
            in_specs=[whole, whole],
            out_specs=pl.BlockSpec((share, r, 2 * width), lambda i, ids: (i, 0, 0)),
        ),
        compiler_params=pltpu.CompilerParams(vmem_limit_bytes=24 * MIB),
        name="gather_rows",
    )(ids, w_gate, w_up)


def block_compute(tokens, tokens_t, d_hidden, weights):
    rows, model = tokens.shape
    width = d_hidden.shape[1]
    n_rows, n_model = 4, 4
    tr, tm = rows // n_rows, model // n_model

    def body(x, xt, dh, w, h_out, d_out, part_out, dd):
        i = pl.program_id(0)

        @pl.when(i < n_rows)
        def _():
            pre = jnp.dot(x[...], w[...], preferred_element_type=F32)
            gate, up = pre[:, :width], pre[:, width:]
            sig = jax.nn.sigmoid(gate)
            act = gate * sig
            h_out[...] = (act * up).astype(BF16)
            g = dh[...].astype(F32)
            at = pl.ds(pl.multiple_of(i * tr, tr), tr)
            dg = (g * up * sig * (1.0 + gate * (1.0 - sig))).astype(BF16)
            du = (g * act).astype(BF16)
            dd[at, :width] = dg
            dd[at, width:] = du
            d_out[:, :width] = dg
            d_out[:, width:] = du

        @pl.when(i >= n_rows)
        def _():
            part_out[...] = jnp.dot(xt[...], dd[...], preferred_element_type=F32).astype(BF16)

    def early(i):
        return jnp.minimum(i, n_rows - 1)

    def late(i):
        return jnp.maximum(i - n_rows, 0)

    return pl.pallas_call(
        body,
        out_shape=[
            jax.ShapeDtypeStruct((rows, width), BF16),
            jax.ShapeDtypeStruct((rows, 2 * width), BF16),
            jax.ShapeDtypeStruct((model, 2 * width), BF16),
        ],
        grid=(n_rows + n_model,),
        in_specs=[
            pl.BlockSpec((tr, model), lambda i: (early(i), 0)),
            pl.BlockSpec((tm, rows), lambda i: (late(i), 0)),
            pl.BlockSpec((tr, width), lambda i: (early(i), 0)),
            pl.BlockSpec((model, 2 * width), lambda i: (0, 0)),
        ],
        out_specs=[
            pl.BlockSpec((tr, width), lambda i: (early(i), 0)),
            pl.BlockSpec((tr, 2 * width), lambda i: (early(i), 0)),
            pl.BlockSpec((tm, 2 * width), lambda i: (late(i), 0)),
        ],
        scratch_shapes=[pltpu.VMEM((rows, 2 * width), BF16)],
        compiler_params=pltpu.CompilerParams(vmem_limit_bytes=40 * MIB),
        cost_estimate=pl.CostEstimate(
            flops=8 * rows * model * width, bytes_accessed=20 * MIB, transcendentals=rows * width
        ),
        name="block_compute",
    )(tokens, tokens_t, d_hidden, weights)


def token_gradient(d_both, weights):
    rows, deep = d_both.shape
    model = weights.shape[0]
    tile = min(256, model)

    def body(d, w, out):
        out[...] = lax.dot_general(
            d[...], w[...], (((1,), (1,)), ((), ())), preferred_element_type=F32
        ).astype(BF16)

    return pl.pallas_call(
        body,
        out_shape=jax.ShapeDtypeStruct((rows, model), BF16),
        grid=(model // tile,),
        in_specs=[pl.BlockSpec((rows, deep), lambda i: (0, 0)), pl.BlockSpec((tile, deep), lambda i: (i, 0))],
        out_specs=pl.BlockSpec((rows, tile), lambda i: (0, i)),
        compiler_params=pltpu.CompilerParams(vmem_limit_bytes=24 * MIB),
        cost_estimate=pl.CostEstimate(flops=2 * rows * model * deep, bytes_accessed=10 * MIB, transcendentals=0),
        name="token_gradient",
    )(d_both, weights)


def sum_terms(ids, terms, experts, width, scale):
    blocks, r, _ = terms.shape
    steps = 3
    w = width // steps

    def body(ids, gate, up, gate_out, up_out, gate_sum, up_sum):
        gate_sum[...] = jnp.zeros_like(gate_sum)
        up_sum[...] = jnp.zeros_like(up_sum)

        def one(b):
            j = ids[b]
            gate_sum[j] = gate_sum[j] + gate[b].astype(F32)
            up_sum[j] = up_sum[j] + up[b].astype(F32)

        each(blocks, one, 4)
        gate_out[...] = (gate_sum[...] * scale).astype(BF16)
        up_out[...] = (up_sum[...] * scale).astype(BF16)

    def cols(n, first):
        return pl.BlockSpec((n, r, w), lambda i, ids: (0, 0, first + i))

    return pl.pallas_call(
        body,
        out_shape=[jax.ShapeDtypeStruct((experts, r, width), BF16)] * 2,
        grid_spec=pltpu.PrefetchScalarGridSpec(
            num_scalar_prefetch=1,
            grid=(steps,),
            in_specs=[cols(blocks, 0), cols(blocks, steps)],
            out_specs=[cols(experts, 0)] * 2,
            scratch_shapes=[pltpu.VMEM((experts, r, w), F32)] * 2,
        ),
        compiler_params=pltpu.CompilerParams(vmem_limit_bytes=24 * MIB),
        name="sum_terms",
    )(ids, terms, terms)


def exchange(parts):
    return lax.all_to_all(parts, BOTH, split_axis=0, concat_axis=0, tiled=True)


def per_device(tokens, d_hidden, w_gate, w_up, expert_ids):
    experts, r, width = w_gate.shape
    blocks = expert_ids.shape[0]
    model = blocks * r
    weights = exchange(gather_rows(expert_ids, w_gate, w_up)).reshape(model, 2 * width)
    tokens_t = lax.optimization_barrier(tokens.T)
    hidden, d_both, part = block_compute(tokens, tokens_t, d_hidden, weights)
    terms = exchange(part.reshape(blocks, r, 2 * width))
    token_grad = token_gradient(d_both, weights)
    grad_gate, grad_up = sum_terms(expert_ids, terms, experts, width, tokens.shape[0] ** (-0.5))
    return hidden, token_grad, grad_gate, grad_up


def solution(mesh):
    rows, weights = P(BOTH, None), P(None, BOTH, None)
    return jax.shard_map(
        per_device,
        mesh=mesh,
        in_specs=(rows, rows, weights, weights, P()),
        out_specs=(rows, rows, weights, weights),
        check_vma=False,
    )
```

```python
import jax
import jax.numpy as jnp
from jax import lax
from jax.experimental import pallas as pl
from jax.experimental.pallas import tpu as pltpu
from jax.sharding import PartitionSpec as P

BOTH = ("expert", "replica")
F32, BF16 = jnp.float32, jnp.bfloat16
MIB = 1 << 20


def each(n, body, unroll=1):
    def step(s, carry):
        body(s)
        return carry

    lax.fori_loop(0, n, step, 0, unroll=unroll)


ANY = pl.BlockSpec(memory_space=pl.ANY)


def gather_rows(ids, w_gate, w_up):
    experts, r, width = w_gate.shape
    blocks = ids.shape[0]
    pieces = 8
    share, lot = blocks // pieces, experts // 4

    def body(ids, gate_hbm, up_hbm, out_hbm, gate, up, out, in_sems, out_sems):
        def arrivals():
            for q in range(4):
                at = pl.ds(q * lot, lot)
                yield pltpu.make_async_copy(gate_hbm.at[at], gate.at[at], in_sems.at[q])
                yield pltpu.make_async_copy(up_hbm.at[at], up.at[at], in_sems.at[4 + q])

        for copy in arrivals():
            copy.start()
        for copy in arrivals():
            copy.wait()

        def leave(p):
            at = pl.ds(p * share, share)
            return pltpu.make_async_copy(out.at[at], out_hbm.at[at], out_sems.at[p])

        for p in range(pieces):
            def one(b):
                j = ids[p * share + b]
                out[p * share + b, :, :width] = gate[j]
                out[p * share + b, :, width:] = up[j]

            each(share, one, 8)
            leave(p).start()
        for p in range(pieces):
            leave(p).wait()

    return pl.pallas_call(
        body,
        out_shape=jax.ShapeDtypeStruct((blocks, r, 2 * width), BF16),
        grid_spec=pltpu.PrefetchScalarGridSpec(
            num_scalar_prefetch=1,
            grid=(1,),
            in_specs=[ANY, ANY],
            out_specs=ANY,
            scratch_shapes=[
                pltpu.VMEM((experts, r, width), BF16),
                pltpu.VMEM((experts, r, width), BF16),
                pltpu.VMEM((blocks, r, 2 * width), BF16),
                pltpu.SemaphoreType.DMA((8,)),
                pltpu.SemaphoreType.DMA((pieces,)),
            ],
        ),
        compiler_params=pltpu.CompilerParams(vmem_limit_bytes=60 * MIB),
        name="gather_rows",
    )(ids, w_gate, w_up)


def block_compute(tokens, tokens_t, d_hidden, weights):
    rows, model = tokens.shape
    width = d_hidden.shape[1]
    n = 4
    tile = model // n
    tr, tc = 32, 256

    def body(x_hbm, xt_hbm, dh_hbm, w_hbm, h_hbm, d_hbm, part_hbm, x, xt, dh, w, h, d, part, pre, in_sems, w_sems, out_sems, part_sems):
        def weight(k):
            at = pl.ds(k * tile, tile)
            return pltpu.make_async_copy(w_hbm.at[at], w.at[at], w_sems.at[k])

        get_x = pltpu.make_async_copy(x_hbm, x, in_sems.at[0])
        get_dh = pltpu.make_async_copy(dh_hbm, dh, in_sems.at[1])
        get_xt = pltpu.make_async_copy(xt_hbm, xt, in_sems.at[2])
        get_x.start()
        for k in range(n):
            weight(k).start()
        get_dh.start()
        get_xt.start()
        get_x.wait()
        for k in range(n):
            weight(k).wait()
            at = pl.ds(k * tile, tile)
            term = jnp.dot(x[:, k * tile : (k + 1) * tile], w[at, :], preferred_element_type=F32)
            if k:
                pre[...] += term
            else:
                pre[...] = term
        get_dh.wait()

        @pl.loop(0, rows // tr)
        def _(k):
            at = pl.ds(pl.multiple_of(k * tr, tr), tr)
            for c in range(0, width, tc):
                gate, up = pre[at, c : c + tc], pre[at, width + c : width + c + tc]
                sig = jax.nn.sigmoid(gate)
                act = gate * sig
                g = dh[at, c : c + tc].astype(F32)
                h[at, c : c + tc] = (act * up).astype(BF16)
                d[at, c : c + tc] = (g * up * sig * (1.0 + gate * (1.0 - sig))).astype(BF16)
                d[at, width + c : width + c + tc] = (g * act).astype(BF16)

        put_h = pltpu.make_async_copy(h, h_hbm, out_sems.at[0])
        put_d = pltpu.make_async_copy(d, d_hbm, out_sems.at[1])
        get_xt.wait()

        def term_out(k):
            at = pl.ds(k * tile, tile)
            return pltpu.make_async_copy(part.at[at], part_hbm.at[at], part_sems.at[k])

        for k in range(n):
            at = pl.ds(k * tile, tile)
            part[at, :] = jnp.dot(xt[at, :], d[...], preferred_element_type=F32).astype(BF16)
            term_out(k).start()
        put_h.start()
        put_d.start()
        for k in range(n):
            term_out(k).wait()
        put_h.wait()
        put_d.wait()

    outs = [(rows, width), (rows, 2 * width), (model, 2 * width)]
    return pl.pallas_call(
        body,
        out_shape=[jax.ShapeDtypeStruct(o, BF16) for o in outs],
        in_specs=[ANY] * 4,
        out_specs=[ANY] * 3,
        scratch_shapes=[
            pltpu.VMEM((rows, model), BF16),
            pltpu.VMEM((model, rows), BF16),
            pltpu.VMEM((rows, width), BF16),
            pltpu.VMEM((model, 2 * width), BF16),
            *[pltpu.VMEM(o, BF16) for o in outs],
            pltpu.VMEM((rows, 2 * width), F32),
            pltpu.SemaphoreType.DMA((3,)),
            pltpu.SemaphoreType.DMA((n,)),
            pltpu.SemaphoreType.DMA((2,)),
            pltpu.SemaphoreType.DMA((n,)),
        ],
        compiler_params=pltpu.CompilerParams(vmem_limit_bytes=60 * MIB),
        cost_estimate=pl.CostEstimate(
            flops=8 * rows * model * width, bytes_accessed=20 * MIB, transcendentals=rows * width
        ),
        name="block_compute",
    )(tokens, tokens_t, d_hidden, weights)


def token_gradient(d_both, weights):
    rows, deep = d_both.shape
    model = weights.shape[0]
    tile = min(256, model)

    def body(d, w, out):
        out[...] = lax.dot_general(
            d[...], w[...], (((1,), (1,)), ((), ())), preferred_element_type=F32
        ).astype(BF16)

    return pl.pallas_call(
        body,
        out_shape=jax.ShapeDtypeStruct((rows, model), BF16),
        grid=(model // tile,),
        in_specs=[pl.BlockSpec((rows, deep), lambda i: (0, 0)), pl.BlockSpec((tile, deep), lambda i: (i, 0))],
        out_specs=pl.BlockSpec((rows, tile), lambda i: (0, i)),
        compiler_params=pltpu.CompilerParams(vmem_limit_bytes=60 * MIB),
        cost_estimate=pl.CostEstimate(flops=2 * rows * model * deep, bytes_accessed=10 * MIB, transcendentals=0),
        name="token_gradient",
    )(d_both, weights)


def sum_terms(ids, terms, experts, width, scale):
    blocks, r, _ = terms.shape
    pieces, lots = 8, 4
    share, lot = blocks // pieces, experts // lots

    def body(ids, term_hbm, gate_hbm, up_hbm, term, total, gate, up, in_sems, gate_sems, up_sems):
        def arrive(p):
            at = pl.ds(p * share, share)
            return pltpu.make_async_copy(term_hbm.at[at], term.at[at], in_sems.at[p])

        for p in range(pieces):
            arrive(p).start()
        total[...] = jnp.zeros_like(total)
        for p in range(pieces):
            arrive(p).wait()

            def one(b):
                j = ids[p * share + b]
                total[j] = total[j] + term[p * share + b].astype(F32)

            each(share, one, 4)

        def leave(q):
            at = pl.ds(q * lot, lot)
            return (
                pltpu.make_async_copy(gate.at[at], gate_hbm.at[at], gate_sems.at[q]),
                pltpu.make_async_copy(up.at[at], up_hbm.at[at], up_sems.at[q]),
            )

        for q in range(lots):
            def out(j):
                gate[q * lot + j] = (total[q * lot + j, :, :width] * scale).astype(BF16)
                up[q * lot + j] = (total[q * lot + j, :, width:] * scale).astype(BF16)

            each(lot, out, 4)
            for copy in leave(q):
                copy.start()
        for q in range(lots):
            for copy in leave(q):
                copy.wait()

    return pl.pallas_call(
        body,
        out_shape=[jax.ShapeDtypeStruct((experts, r, width), BF16)] * 2,
        grid_spec=pltpu.PrefetchScalarGridSpec(
            num_scalar_prefetch=1,
            grid=(1,),
            in_specs=[ANY],
            out_specs=[ANY] * 2,
            scratch_shapes=[
                pltpu.VMEM((blocks, r, 2 * width), BF16),
                pltpu.VMEM((experts, r, 2 * width), F32),
                pltpu.VMEM((experts, r, width), BF16),
                pltpu.VMEM((experts, r, width), BF16),
                pltpu.SemaphoreType.DMA((pieces,)),
                pltpu.SemaphoreType.DMA((lots,)),
                pltpu.SemaphoreType.DMA((lots,)),
            ],
        ),
        compiler_params=pltpu.CompilerParams(vmem_limit_bytes=60 * MIB),
        name="sum_terms",
    )(ids, terms)


def exchange(parts):
    return lax.all_to_all(parts, BOTH, split_axis=0, concat_axis=0, tiled=True)


def per_device(tokens, d_hidden, w_gate, w_up, expert_ids):
    experts, r, width = w_gate.shape
    blocks = expert_ids.shape[0]
    model = blocks * r
    weights = exchange(gather_rows(expert_ids, w_gate, w_up)).reshape(model, 2 * width)
    tokens_t = lax.optimization_barrier(tokens.T)
    hidden, d_both, part = block_compute(tokens, tokens_t, d_hidden, weights)
    terms = exchange(part.reshape(blocks, r, 2 * width))
    token_grad = token_gradient(d_both, weights)
    grad_gate, grad_up = sum_terms(expert_ids, terms, experts, width, tokens.shape[0] ** (-0.5))
    return hidden, token_grad, grad_gate, grad_up


def solution(mesh):
    rows, weights = P(BOTH, None), P(None, BOTH, None)
    return jax.shard_map(
        per_device,
        mesh=mesh,
        in_specs=(rows, rows, weights, weights, P()),
        out_specs=(rows, rows, weights, weights),
        check_vma=False,
    )
```

```python
import jax
import jax.numpy as jnp
from jax import lax
from jax.experimental import pallas as pl
from jax.experimental.pallas import tpu as pltpu
from jax.sharding import PartitionSpec as P

BOTH = ("expert", "replica")
F32, BF16 = jnp.float32, jnp.bfloat16
MIB = 1 << 20


def each(n, body, unroll=1):
    def step(s, carry):
        body(s)
        return carry

    lax.fori_loop(0, n, step, 0, unroll=unroll)


ANY = pl.BlockSpec(memory_space=pl.ANY)


def gather_rows(ids, w_gate, w_up):
    experts, r, width = w_gate.shape
    blocks = ids.shape[0]
    pieces = 8
    share, lot = blocks // pieces, experts // 4

    def body(ids, gate_hbm, up_hbm, out_hbm, gate, up, out, in_sems, out_sems):
        def arrival(source, target, first, q):
            at = pl.ds(q * lot, lot)
            return pltpu.make_async_copy(source.at[at], target.at[at], in_sems.at[first + q])

        for q in range(4):
            arrival(gate_hbm, gate, 0, q).start()
        for q in range(4):
            arrival(up_hbm, up, 4, q).start()
        for q in range(4):
            arrival(gate_hbm, gate, 0, q).wait()

        def gate_half(b):
            out[b, :, :width] = gate[ids[b]]

        each(blocks, gate_half, 8)
        for q in range(4):
            arrival(up_hbm, up, 4, q).wait()

        def leave(p):
            at = pl.ds(p * share, share)
            return pltpu.make_async_copy(out.at[at], out_hbm.at[at], out_sems.at[p])

        for p in range(pieces):
            def one(b):
                out[p * share + b, :, width:] = up[ids[p * share + b]]

            each(share, one, 8)
            leave(p).start()
        for p in range(pieces):
            leave(p).wait()

    return pl.pallas_call(
        body,
        out_shape=jax.ShapeDtypeStruct((blocks, r, 2 * width), BF16),
        grid_spec=pltpu.PrefetchScalarGridSpec(
            num_scalar_prefetch=1,
            grid=(1,),
            in_specs=[ANY, ANY],
            out_specs=ANY,
            scratch_shapes=[
                pltpu.VMEM((experts, r, width), BF16),
                pltpu.VMEM((experts, r, width), BF16),
                pltpu.VMEM((blocks, r, 2 * width), BF16),
                pltpu.SemaphoreType.DMA((8,)),
                pltpu.SemaphoreType.DMA((pieces,)),
            ],
        ),
        compiler_params=pltpu.CompilerParams(vmem_limit_bytes=60 * MIB),
        name="gather_rows",
    )(ids, w_gate, w_up)


def block_compute(tokens, tokens_t, d_hidden, weights):
    rows, model = tokens.shape
    width = d_hidden.shape[1]
    n, pieces = 4, 8
    tile, piece = model // n, model // pieces
    tr, tc = 32, 256

    def body(x_hbm, xt_hbm, dh_hbm, w_hbm, h_hbm, d_hbm, part_hbm, x, xt, dh, w, h, d, part, pre, in_sems, x_sems, w_sems, out_sems, part_sems):
        def weight(k):
            at = pl.ds(k * tile, tile)
            return pltpu.make_async_copy(w_hbm.at[at], w.at[at], w_sems.at[k])

        def columns(k):
            at = pl.ds(k * tile, tile)
            return pltpu.make_async_copy(x_hbm.at[:, at], x.at[:, at], x_sems.at[k])

        get_dh = pltpu.make_async_copy(dh_hbm, dh, in_sems.at[0])
        get_xt = pltpu.make_async_copy(xt_hbm, xt, in_sems.at[1])
        for k in range(n):
            columns(k).start()
            weight(k).start()
        get_dh.start()
        get_xt.start()
        for k in range(n):
            columns(k).wait()
            weight(k).wait()
            at = pl.ds(k * tile, tile)
            term = jnp.dot(x[:, k * tile : (k + 1) * tile], w[at, :], preferred_element_type=F32)
            if k:
                pre[...] += term
            else:
                pre[...] = term
        get_dh.wait()

        @pl.loop(0, rows // tr)
        def _(k):
            at = pl.ds(pl.multiple_of(k * tr, tr), tr)
            for c in range(0, width, tc):
                gate, up = pre[at, c : c + tc], pre[at, width + c : width + c + tc]
                sig = jax.nn.sigmoid(gate)
                act = gate * sig
                g = dh[at, c : c + tc].astype(F32)
                h[at, c : c + tc] = (act * up).astype(BF16)
                d[at, c : c + tc] = (g * up * sig * (1.0 + gate * (1.0 - sig))).astype(BF16)
                d[at, width + c : width + c + tc] = (g * act).astype(BF16)

        put_h = pltpu.make_async_copy(h, h_hbm, out_sems.at[0])
        put_d = pltpu.make_async_copy(d, d_hbm, out_sems.at[1])
        put_h.start()
        put_d.start()
        get_xt.wait()

        def term_out(k):
            at = pl.ds(k * piece, piece)
            return pltpu.make_async_copy(part.at[at], part_hbm.at[at], part_sems.at[k])

        for k in range(pieces):
            at = pl.ds(k * piece, piece)
            part[at, :] = jnp.dot(xt[at, :], d[...], preferred_element_type=F32).astype(BF16)
            term_out(k).start()
        for k in range(pieces):
            term_out(k).wait()
        put_h.wait()
        put_d.wait()

    outs = [(rows, width), (rows, 2 * width), (model, 2 * width)]
    return pl.pallas_call(
        body,
        out_shape=[jax.ShapeDtypeStruct(o, BF16) for o in outs],
        in_specs=[ANY] * 4,
        out_specs=[ANY] * 3,
        scratch_shapes=[
            pltpu.VMEM((rows, model), BF16),
            pltpu.VMEM((model, rows), BF16),
            pltpu.VMEM((rows, width), BF16),
            pltpu.VMEM((model, 2 * width), BF16),
            *[pltpu.VMEM(o, BF16) for o in outs],
            pltpu.VMEM((rows, 2 * width), F32),
            pltpu.SemaphoreType.DMA((2,)),
            pltpu.SemaphoreType.DMA((n,)),
            pltpu.SemaphoreType.DMA((n,)),
            pltpu.SemaphoreType.DMA((2,)),
            pltpu.SemaphoreType.DMA((pieces,)),
        ],
        compiler_params=pltpu.CompilerParams(vmem_limit_bytes=60 * MIB),
        cost_estimate=pl.CostEstimate(
            flops=8 * rows * model * width, bytes_accessed=20 * MIB, transcendentals=rows * width
        ),
        name="block_compute",
    )(tokens, tokens_t, d_hidden, weights)


def token_gradient(d_both, weights):
    rows, deep = d_both.shape
    model = weights.shape[0]
    tile = min(256, model)

    def body(d, w, out):
        out[...] = lax.dot_general(
            d[...], w[...], (((1,), (1,)), ((), ())), preferred_element_type=F32
        ).astype(BF16)

    return pl.pallas_call(
        body,
        out_shape=jax.ShapeDtypeStruct((rows, model), BF16),
        grid=(model // tile,),
        in_specs=[pl.BlockSpec((rows, deep), lambda i: (0, 0)), pl.BlockSpec((tile, deep), lambda i: (i, 0))],
        out_specs=pl.BlockSpec((rows, tile), lambda i: (0, i)),
        compiler_params=pltpu.CompilerParams(vmem_limit_bytes=60 * MIB),
        cost_estimate=pl.CostEstimate(flops=2 * rows * model * deep, bytes_accessed=10 * MIB, transcendentals=0),
        name="token_gradient",
    )(d_both, weights)


def sum_terms(ids, terms, experts, width, scale):
    blocks, r, _ = terms.shape
    pieces, lots = 8, 4
    share, lot = blocks // pieces, experts // lots

    def body(ids, term_hbm, gate_hbm, up_hbm, term, total, gate, up, in_sems, gate_sems, up_sems):
        def arrive(p):
            at = pl.ds(p * share, share)
            return pltpu.make_async_copy(term_hbm.at[at], term.at[at], in_sems.at[p])

        for p in range(pieces):
            arrive(p).start()
        total[...] = jnp.zeros_like(total)
        for p in range(pieces):
            arrive(p).wait()

            def one(b):
                j = ids[p * share + b]
                total[j] = total[j] + term[p * share + b].astype(F32)

            each(share, one, 4)

        def leave(q):
            at = pl.ds(q * lot, lot)
            return (
                pltpu.make_async_copy(gate.at[at], gate_hbm.at[at], gate_sems.at[q]),
                pltpu.make_async_copy(up.at[at], up_hbm.at[at], up_sems.at[q]),
            )

        for q in range(lots):
            def out(j):
                gate[q * lot + j] = (total[q * lot + j, :, :width] * scale).astype(BF16)
                up[q * lot + j] = (total[q * lot + j, :, width:] * scale).astype(BF16)

            each(lot, out, 4)
            for copy in leave(q):
                copy.start()
        for q in range(lots):
            for copy in leave(q):
                copy.wait()

    return pl.pallas_call(
        body,
        out_shape=[jax.ShapeDtypeStruct((experts, r, width), BF16)] * 2,
        grid_spec=pltpu.PrefetchScalarGridSpec(
            num_scalar_prefetch=1,
            grid=(1,),
            in_specs=[ANY],
            out_specs=[ANY] * 2,
            scratch_shapes=[
                pltpu.VMEM((blocks, r, 2 * width), BF16),
                pltpu.VMEM((experts, r, 2 * width), F32),
                pltpu.VMEM((experts, r, width), BF16),
                pltpu.VMEM((experts, r, width), BF16),
                pltpu.SemaphoreType.DMA((pieces,)),
                pltpu.SemaphoreType.DMA((lots,)),
                pltpu.SemaphoreType.DMA((lots,)),
            ],
        ),
        compiler_params=pltpu.CompilerParams(vmem_limit_bytes=60 * MIB),
        name="sum_terms",
    )(ids, terms)


def exchange(parts):
    return lax.all_to_all(parts, BOTH, split_axis=0, concat_axis=0, tiled=True)


def per_device(tokens, d_hidden, w_gate, w_up, expert_ids):
    experts, r, width = w_gate.shape
    blocks = expert_ids.shape[0]
    model = blocks * r
    weights = exchange(gather_rows(expert_ids, w_gate, w_up)).reshape(model, 2 * width)
    tokens_t = lax.optimization_barrier(tokens.T)
    hidden, d_both, part = block_compute(tokens, tokens_t, d_hidden, weights)
    terms = exchange(part.reshape(blocks, r, 2 * width))
    token_grad = token_gradient(d_both, weights)
    grad_gate, grad_up = sum_terms(expert_ids, terms, experts, width, tokens.shape[0] ** (-0.5))
    return hidden, token_grad, grad_gate, grad_up


def solution(mesh):
    rows, weights = P(BOTH, None), P(None, BOTH, None)
    return jax.shard_map(
        per_device,
        mesh=mesh,
        in_specs=(rows, rows, weights, weights, P()),
        out_specs=(rows, rows, weights, weights),
        check_vma=False,
    )
```

```python
import jax
import jax.numpy as jnp
from jax import lax
from jax.experimental import pallas as pl
from jax.experimental.pallas import tpu as pltpu
from jax.sharding import PartitionSpec as P

BOTH = ("expert", "replica")
F32, BF16 = jnp.float32, jnp.bfloat16
MIB = 1 << 20


def each(n, body, unroll=1):
    def step(s, carry):
        body(s)
        return carry

    lax.fori_loop(0, n, step, 0, unroll=unroll)


ANY = pl.BlockSpec(memory_space=pl.ANY)


def gather_rows(ids, w_gate, w_up):
    experts, r, width = w_gate.shape
    blocks = ids.shape[0]
    pieces = 8
    share, lot = blocks // pieces, experts // 4

    def body(ids, gate_hbm, up_hbm, out_hbm, gate, up, out, in_sems, out_sems):
        def arrival(source, target, first, q):
            at = pl.ds(q * lot, lot)
            return pltpu.make_async_copy(source.at[at], target.at[at], in_sems.at[first + q])

        for q in range(4):
            arrival(gate_hbm, gate, 0, q).start()
        for q in range(4):
            arrival(up_hbm, up, 4, q).start()
        for q in range(4):
            arrival(gate_hbm, gate, 0, q).wait()

        def gate_half(b):
            out[b, :, :width] = gate[ids[b]]

        each(blocks, gate_half, 8)
        for q in range(4):
            arrival(up_hbm, up, 4, q).wait()

        def leave(p):
            at = pl.ds(p * share, share)
            return pltpu.make_async_copy(out.at[at], out_hbm.at[at], out_sems.at[p])

        for p in range(pieces):
            def one(b):
                out[p * share + b, :, width:] = up[ids[p * share + b]]

            each(share, one, 8)
            leave(p).start()
        for p in range(pieces):
            leave(p).wait()

    return pl.pallas_call(
        body,
        out_shape=jax.ShapeDtypeStruct((blocks, r, 2 * width), BF16),
        grid_spec=pltpu.PrefetchScalarGridSpec(
            num_scalar_prefetch=1,
            grid=(1,),
            in_specs=[ANY, ANY],
            out_specs=ANY,
            scratch_shapes=[
                pltpu.VMEM((experts, r, width), BF16),
                pltpu.VMEM((experts, r, width), BF16),
                pltpu.VMEM((blocks, r, 2 * width), BF16),
                pltpu.SemaphoreType.DMA((8,)),
                pltpu.SemaphoreType.DMA((pieces,)),
            ],
        ),
        compiler_params=pltpu.CompilerParams(vmem_limit_bytes=60 * MIB),
        name="gather_rows",
    )(ids, w_gate, w_up)


def block_compute(tokens, tokens_t, d_hidden, weights):
    rows, model = tokens.shape
    width = d_hidden.shape[1]
    n, pieces = 4, 8
    tile, piece = model // n, model // pieces
    tr, tc = 32, 256

    def body(x_hbm, xt_hbm, dh_hbm, w_hbm, h_hbm, d_hbm, part_hbm, x, xt, dh, w, h, d, part, pre, in_sems, x_sems, w_sems, out_sems, part_sems):
        def weight(k):
            at = pl.ds(k * tile, tile)
            return pltpu.make_async_copy(w_hbm.at[at], w.at[at], w_sems.at[k])

        def columns(k):
            at = pl.ds(k * tile, tile)
            return pltpu.make_async_copy(x_hbm.at[:, at], x.at[:, at], x_sems.at[k])

        get_dh = pltpu.make_async_copy(dh_hbm, dh, in_sems.at[0])
        get_xt = pltpu.make_async_copy(xt_hbm, xt, in_sems.at[1])
        for k in range(n):
            columns(k).start()
            weight(k).start()
        get_dh.start()
        get_xt.start()
        for k in range(n):
            columns(k).wait()
            weight(k).wait()
            at = pl.ds(k * tile, tile)
            term = jnp.dot(x[:, k * tile : (k + 1) * tile], w[at, :], preferred_element_type=F32)
            if k:
                pre[...] += term
            else:
                pre[...] = term
        get_dh.wait()

        @pl.loop(0, rows // tr)
        def _(k):
            at = pl.ds(pl.multiple_of(k * tr, tr), tr)
            for c in range(0, width, tc):
                gate, up = pre[at, c : c + tc], pre[at, width + c : width + c + tc]
                sig = jax.nn.sigmoid(gate)
                act = gate * sig
                g = dh[at, c : c + tc].astype(F32)
                h[at, c : c + tc] = (act * up).astype(BF16)
                d[at, c : c + tc] = (g * up * sig * (1.0 + gate * (1.0 - sig))).astype(BF16)
                d[at, width + c : width + c + tc] = (g * act).astype(BF16)

        put_h = pltpu.make_async_copy(h, h_hbm, out_sems.at[0])
        put_d = pltpu.make_async_copy(d, d_hbm, out_sems.at[1])
        put_h.start()
        put_d.start()
        get_xt.wait()

        def term_out(k):
            at = pl.ds(k * piece, piece)
            return pltpu.make_async_copy(part.at[at], part_hbm.at[at], part_sems.at[k])

        for k in range(pieces):
            at = pl.ds(k * piece, piece)
            part[at, :] = jnp.dot(xt[at, :], d[...], preferred_element_type=F32).astype(BF16)
            term_out(k).start()
        for k in range(pieces):
            term_out(k).wait()
        put_h.wait()
        put_d.wait()

    outs = [(rows, width), (rows, 2 * width), (model, 2 * width)]
    return pl.pallas_call(
        body,
        out_shape=[jax.ShapeDtypeStruct(o, BF16) for o in outs],
        in_specs=[ANY] * 4,
        out_specs=[ANY] * 3,
        scratch_shapes=[
            pltpu.VMEM((rows, model), BF16),
            pltpu.VMEM((model, rows), BF16),
            pltpu.VMEM((rows, width), BF16),
            pltpu.VMEM((model, 2 * width), BF16),
            *[pltpu.VMEM(o, BF16) for o in outs],
            pltpu.VMEM((rows, 2 * width), F32),
            pltpu.SemaphoreType.DMA((2,)),
            pltpu.SemaphoreType.DMA((n,)),
            pltpu.SemaphoreType.DMA((n,)),
            pltpu.SemaphoreType.DMA((2,)),
            pltpu.SemaphoreType.DMA((pieces,)),
        ],
        compiler_params=pltpu.CompilerParams(vmem_limit_bytes=60 * MIB),
        cost_estimate=pl.CostEstimate(
            flops=8 * rows * model * width, bytes_accessed=20 * MIB, transcendentals=rows * width
        ),
        name="block_compute",
    )(tokens, tokens_t, d_hidden, weights)


def token_gradient(d_both, weights):
    rows, deep = d_both.shape
    model = weights.shape[0]
    tile = min(256, model)

    def body(d, w, out):
        out[...] = lax.dot_general(
            d[...], w[...], (((1,), (1,)), ((), ())), preferred_element_type=F32
        ).astype(BF16)

    return pl.pallas_call(
        body,
        out_shape=jax.ShapeDtypeStruct((rows, model), BF16),
        grid=(model // tile,),
        in_specs=[pl.BlockSpec((rows, deep), lambda i: (0, 0)), pl.BlockSpec((tile, deep), lambda i: (i, 0))],
        out_specs=pl.BlockSpec((rows, tile), lambda i: (0, i)),
        compiler_params=pltpu.CompilerParams(vmem_limit_bytes=60 * MIB),
        cost_estimate=pl.CostEstimate(flops=2 * rows * model * deep, bytes_accessed=10 * MIB, transcendentals=0),
        name="token_gradient",
    )(d_both, weights)


def sum_terms(ids, terms, experts, width, scale):
    blocks, r, _ = terms.shape
    pieces, lots = 8, 4
    share, lot = blocks // pieces, experts // lots

    def body(ids, term_hbm, gate_hbm, up_hbm, term, total, other, gate, up, in_sems, gate_sems, up_sems):
        def arrive(p):
            at = pl.ds(p * share, share)
            return pltpu.make_async_copy(term_hbm.at[at], term.at[at], in_sems.at[p])

        for p in range(pieces):
            arrive(p).start()
        total[...] = jnp.zeros_like(total)
        other[...] = jnp.zeros_like(other)
        for p in range(pieces):
            arrive(p).wait()

            def one(b):
                even = p * share + 2 * b
                j, k = ids[even], ids[even + 1]
                first = total[j] + term[even].astype(F32)
                second = other[k] + term[even + 1].astype(F32)
                total[j] = first
                other[k] = second

            each(share // 2, one, 4)

        def leave(q):
            at = pl.ds(q * lot, lot)
            return (
                pltpu.make_async_copy(gate.at[at], gate_hbm.at[at], gate_sems.at[q]),
                pltpu.make_async_copy(up.at[at], up_hbm.at[at], up_sems.at[q]),
            )

        for q in range(lots):
            def out(j):
                grad = (total[q * lot + j] + other[q * lot + j]) * scale
                gate[q * lot + j] = grad[:, :width].astype(BF16)
                up[q * lot + j] = grad[:, width:].astype(BF16)

            each(lot, out, 4)
            for copy in leave(q):
                copy.start()
        for q in range(lots):
            for copy in leave(q):
                copy.wait()

    return pl.pallas_call(
        body,
        out_shape=[jax.ShapeDtypeStruct((experts, r, width), BF16)] * 2,
        grid_spec=pltpu.PrefetchScalarGridSpec(
            num_scalar_prefetch=1,
            grid=(1,),
            in_specs=[ANY],
            out_specs=[ANY] * 2,
            scratch_shapes=[
                pltpu.VMEM((blocks, r, 2 * width), BF16),
                pltpu.VMEM((experts, r, 2 * width), F32),
                pltpu.VMEM((experts, r, 2 * width), F32),
                pltpu.VMEM((experts, r, width), BF16),
                pltpu.VMEM((experts, r, width), BF16),
                pltpu.SemaphoreType.DMA((pieces,)),
                pltpu.SemaphoreType.DMA((lots,)),
                pltpu.SemaphoreType.DMA((lots,)),
            ],
        ),
        compiler_params=pltpu.CompilerParams(vmem_limit_bytes=60 * MIB),
        name="sum_terms",
    )(ids, terms)


def exchange(parts):
    return lax.all_to_all(parts, BOTH, split_axis=0, concat_axis=0, tiled=True)


def per_device(tokens, d_hidden, w_gate, w_up, expert_ids):
    experts, r, width = w_gate.shape
    blocks = expert_ids.shape[0]
    model = blocks * r
    weights = exchange(gather_rows(expert_ids, w_gate, w_up)).reshape(model, 2 * width)
    tokens_t = lax.optimization_barrier(tokens.T)
    hidden, d_both, part = block_compute(tokens, tokens_t, d_hidden, weights)
    terms = exchange(part.reshape(blocks, r, 2 * width))
    token_grad = token_gradient(d_both, weights)
    grad_gate, grad_up = sum_terms(expert_ids, terms, experts, width, tokens.shape[0] ** (-0.5))
    return hidden, token_grad, grad_gate, grad_up


def solution(mesh):
    rows, weights = P(BOTH, None), P(None, BOTH, None)
    return jax.shard_map(
        per_device,
        mesh=mesh,
        in_specs=(rows, rows, weights, weights, P()),
        out_specs=(rows, rows, weights, weights),
        check_vma=False,
    )
```
